32 devices in a mesh: seq: 16 (over z, y, x), head: 2 (over core).
Axes of the slice: x: 2, y: 2, z: 4, core: 2. Of those that a mesh axis runs over, the one named last changes fastest.
Arguments:
- queries: bfloat16 [2, 3072, 1024], P(None, 'seq', 'head'), may hold values from -160 to 160
- key_rows: bfloat16 [2, 3072, 1024], P(None, 'seq', 'head'), may hold values from -9 to 9
- value_rows: bfloat16 [2, 3072, 1024], P(None, 'seq', 'head'), may hold values from -6 to 6
- hidden_in: bfloat16 [3072, 1024], P('seq', 'head'), may hold values from -6 to 6
- rate_weight: bfloat16 [1024, 6], P('head'), may hold values from -0.5 to 0.5
- first_weight: bfloat16 [2, 512, 512], P('head'), may hold values from -0.25 to 0.25
- down_weight: bfloat16 [2, 512, 512], P('head'), may hold values from -0.25 to 0.25
- third_weight: bfloat16 [2, 512, 512], P('head'), may hold values from -0.25 to 0.25
- out_gain: float32 [1024], P('head'), may hold values from 0.25 to 1.75
Outputs:
- mixed: bfloat16 [2, 3072, 1024], P(None, 'seq', 'head')
The draws below stay inside these ranges and needn't reach their ends.
All inputs are finite; a program needn't handle non-finite values.
Results may differ from the reference program's by a relative error of at most 0.0085.
Values may be sent and summed in bfloat16 or wider, within the bound.
A program may use at most 64 MiB of HBM per device.

```python
import jax
import jax.numpy as jnp
from jax import lax

DH = 512
FH = 512
WINDOW = 512
NS_STEPS = 3
STRETCHES = 2
HEADS = 2
D = 1024
STRETCH = 3072


def paired_rows(key):
    length = STRETCHES * STRETCH
    base_q = jnp.clip(1.5 * jax.random.normal(jax.random.fold_in(key, 11), (length, HEADS, DH), jnp.float32), -9.0, 9.0)
    base_k = jnp.clip(1.5 * jax.random.normal(jax.random.fold_in(key, 12), (length, HEADS, DH), jnp.float32), -9.0, 9.0)
    return (base_q.reshape(STRETCHES, STRETCH, HEADS * DH), base_k.reshape(STRETCHES, STRETCH, HEADS * DH))


def draw_queries(key, part):
    return paired_rows(key)[0].astype(jnp.bfloat16)


def draw_key_rows(key, part):
    return paired_rows(key)[1].astype(jnp.bfloat16)


def raised(result, key, source, target, blocks, factor):
    owner, partner = [(jnp.arange(result.shape[dim]) // (result.shape[dim] // blocks)).reshape([-1 if axis == dim else 1 for axis in range(result.ndim)]) for dim in (source, target)]
    chosen = jax.random.permutation(key, blocks)[partner]
    strong = (owner == chosen) | (owner == (partner + blocks // 2) % blocks)
    return jnp.where(strong, factor * result, result)


def shard_levels(own_key, dims, pieces, least, top_value):
    level, own = 1.0, jax.random.fold_in(own_key, 6)
    for dim, shards_of in pieces:
        steps = jnp.exp(jax.random.uniform(jax.random.fold_in(own, dim), (shards_of,), jnp.float32, least / len(pieces), top_value / len(pieces)))
        level = level * jnp.repeat(steps, dims[dim] // shards_of).reshape([-1 if axis == dim else 1 for axis in range(len(dims))])
    return level


def centred(rng, shape, width, limit, split=(), kind=jnp.bfloat16):
    drawn = jax.random.normal(rng, shape, jnp.float32) * width
    if len(split) > 0:
        drawn = shard_levels(rng, shape, split, -0.22, 0.18) * drawn
    return jnp.clip(drawn, min=-limit, max=limit).astype(kind)


def noise_with(own_key, dims, deviation, reach, split, heavy, kind=jnp.bfloat16):
    entries = deviation * jax.random.normal(own_key, dims, jnp.float32)
    if split:
        entries = entries * shard_levels(own_key, dims, split, -0.22, 0.18)
    return jnp.clip(raised(entries, jax.random.fold_in(own_key, 3), *heavy), -reach, reach).astype(kind)


def setup_inputs(seed: int = 0) -> dict:
    arg_keys = jax.random.split(jax.random.key(seed), 10)
    queries = draw_queries(jax.random.fold_in(arg_keys[9], 71), 0)
    key_rows = draw_key_rows(jax.random.fold_in(arg_keys[9], 71), 0)
    value_rows = centred(arg_keys[2], (STRETCHES, STRETCH, D), 1.0, 6.0, ((1, 16), (2, 2)))
    hidden_in = centred(arg_keys[3], (STRETCH, D), 1.0, 6.0, ((0, 16), (1, 2)))
    rate_weight = noise_with(arg_keys[4], (D, 3 * HEADS), (D // 4) ** -0.5, 0.5, ((0, 2),), (0, 1, 2, 2.0))
    first_weight = centred(arg_keys[5], (HEADS, FH, DH), DH ** -0.5, 0.25, ((0, 2),))
    down_weight = centred(arg_keys[6], (HEADS, DH, FH), FH ** -0.5, 0.25, ((0, 2),))
    third_weight = centred(arg_keys[7], (HEADS, FH, DH), DH ** -0.5, 0.25, ((0, 2),))
    out_gain = jnp.clip(1.0 + 0.15 * jax.random.normal(arg_keys[8], (D,), jnp.float32), 0.25, 1.75)
    return {"queries": queries, "key_rows": key_rows, "value_rows": value_rows, "hidden_in": hidden_in, "rate_weight": rate_weight, "first_weight": first_weight, "down_weight": down_weight, "third_weight": third_weight, "out_gain": out_gain}


step_size = 1.0
norm_floor = 1e-07

def contract_last(left, right):
    return lax.dot_general(left, right, (((1,), (1,)), ((), ())), preferred_element_type=jnp.float32)

def contract_first(left, right):
    return lax.dot_general(left, right, (((0,), (0,)), ((), ())), preferred_element_type=jnp.float32)

def newton_rows(rows_now, whole):
    gram = contract_last(rows_now, whole).astype(jnp.bfloat16)
    product = jnp.dot(gram, whole, preferred_element_type=jnp.float32)
    return (1.5 * rows_now.astype(jnp.float32) - 0.5 * product).astype(jnp.bfloat16)

def normalized(matrix, squares):
    return (matrix / (jnp.sqrt(squares) + norm_floor)).astype(jnp.bfloat16)

def fast_apply(inputs, weight_one, weight_two, weight_three):
    gate_pre = contract_last(inputs, weight_one)
    up_pre = contract_last(inputs, weight_three)
    hidden_act = (jax.nn.silu(gate_pre) * up_pre).astype(jnp.bfloat16)
    return contract_last(hidden_act, weight_two)

def window_attention(q_flat, k_flat, v_flat):
    length = q_flat.shape[0]
    head_size = q_flat.shape[1]
    blocks = length // WINDOW
    pad_keys = jnp.concatenate([jnp.zeros((WINDOW, head_size), k_flat.dtype), k_flat], axis=0)
    pad_values = jnp.concatenate([jnp.zeros((WINDOW, head_size), v_flat.dtype), v_flat], axis=0)
    scale = 1.0 / jnp.sqrt(jnp.float32(head_size))

    def one_block(index):
        start = (index * WINDOW).astype(jnp.int32)
        q_blk = lax.dynamic_slice_in_dim(q_flat, start, WINDOW, 0)
        k_blk = lax.dynamic_slice_in_dim(pad_keys, start, 2 * WINDOW, 0)
        v_blk = lax.dynamic_slice_in_dim(pad_values, start, 2 * WINDOW, 0)
        query_pos = start + jnp.arange(WINDOW).astype(jnp.int32)[:, None]
        key_pos = start - WINDOW + jnp.arange(2 * WINDOW).astype(jnp.int32)[None, :]
        delta = query_pos - key_pos
        allowed = (delta >= 0) & (delta < WINDOW) & (key_pos >= 0)
        scores = contract_last(q_blk, k_blk) * scale
        scores = jnp.where(allowed, scores, jnp.float32(-1e+30))
        top = lax.optimization_barrier(jnp.max(scores, axis=-1, keepdims=True))
        expo = jnp.exp(scores - top)
        probs = (expo / lax.optimization_barrier(jnp.sum(expo, axis=-1, keepdims=True))).astype(jnp.bfloat16)
        return jnp.dot(probs, v_blk, preferred_element_type=jnp.float32)
    return lax.map(one_block, jnp.arange(blocks).astype(jnp.int32)).reshape(length, head_size)

def one_head(packed):
    q_flat, k_flat, v_flat, weight_one, weight_two, weight_three, rates, gain = packed
    key_early = k_flat[:STRETCH]
    value_early = v_flat[:STRETCH]
    gate_pre = contract_last(key_early, weight_one)
    up_pre = contract_last(key_early, weight_three)
    sigmoid_gate = jax.nn.sigmoid(gate_pre)
    gate_act = gate_pre * sigmoid_gate
    hidden_act = (gate_act * up_pre).astype(jnp.bfloat16)
    value_back = jnp.dot(value_early, weight_two, preferred_element_type=jnp.float32)
    scaled_values = (value_early.astype(jnp.float32) * rates[:, 1:2]).astype(jnp.bfloat16)
    gate_back = (rates[:, 0:1] * value_back * up_pre * sigmoid_gate * (1.0 + gate_pre * (1.0 - sigmoid_gate))).astype(jnp.bfloat16)
    up_back = (rates[:, 2:3] * value_back * gate_act).astype(jnp.bfloat16)
    grads = [contract_first(gate_back, key_early), contract_first(scaled_values, hidden_act), contract_first(up_back, key_early)]
    iterates = [normalized(matrix, jnp.sum(matrix * matrix)) for matrix in grads]
    for turn in range(NS_STEPS):
        iterates = [newton_rows(matrix, matrix) for matrix in iterates]
    new_one = (weight_one.astype(jnp.float32) + step_size * iterates[0].astype(jnp.float32)).astype(jnp.bfloat16)
    new_two = (weight_two.astype(jnp.float32) + step_size * iterates[1].astype(jnp.float32)).astype(jnp.bfloat16)
    new_three = (weight_three.astype(jnp.float32) + step_size * iterates[2].astype(jnp.float32)).astype(jnp.bfloat16)
    fast_early = fast_apply(q_flat[:STRETCH], weight_one, weight_two, weight_three)
    fast_late = fast_apply(q_flat[STRETCH:], new_one, new_two, new_three)
    fast = jnp.concatenate([fast_early, fast_late], axis=0)
    normed = fast * lax.rsqrt(lax.optimization_barrier(jnp.mean(fast * fast, axis=-1, keepdims=True)) + 1e-06) * gain
    attended = window_attention(q_flat, k_flat, v_flat)
    return (attended + normed).astype(jnp.bfloat16)

def reference(queries, key_rows, value_rows, hidden_in, rate_weight, first_weight, down_weight, third_weight, out_gain):
    heads = first_weight.shape[0]
    head_size = first_weight.shape[2]

    def per_head(tensor):
        return tensor.reshape(STRETCHES * STRETCH, heads, head_size).transpose(1, 0, 2)
    rates = jax.nn.softplus(jnp.dot(hidden_in, rate_weight, preferred_element_type=jnp.float32))
    rates = rates.reshape(STRETCH, heads, 3).transpose(1, 0, 2)
    gains = out_gain.reshape(heads, head_size)
    mixed = lax.map(one_head, (per_head(queries), per_head(key_rows), per_head(value_rows), first_weight, down_weight, third_weight, rates, gains))
    return mixed.transpose(1, 0, 2).reshape(STRETCHES, STRETCH, heads * head_size)
```

```python
import functools

import jax
import jax.numpy as jnp
from jax import lax
from jax.experimental import pallas as pl
from jax.experimental.pallas import tpu as pltpu
from jax.sharding import PartitionSpec as P

WINDOW = 512
NS_STEPS = 3
LEAST_ROWS = 64
MESH = pl.DeviceIdType.MESH

step_size = 1.0
norm_floor = 1e-07


def contract_last(left, right):
    return lax.dot_general(
        left, right, (((1,), (1,)), ((), ())), preferred_element_type=jnp.float32
    )


def contract_first(left, right):
    return lax.dot_general(
        left, right, (((0,), (0,)), ((), ())), preferred_element_type=jnp.float32
    )


def plan(seq_count, rows):
    bits = seq_count.bit_length() - 1
    turning = min(3, bits)
    orders = []
    for m in range(3):
        first = [(m + s) % turning for s in range(turning)] if turning else []
        orders.append(first + list(range(turning, bits)))
    sizes, held, halving = [], rows, 0
    for _ in range(bits):
        if held // 2 >= LEAST_ROWS:
            held //= 2
            halving += 1
        sizes.append(held)
    return orders, sizes, halving


def kernel(
    shape,
    q_ref,
    k_ref,
    v_ref,
    hid_ref,
    rw_ref,
    w1_ref,
    w2_ref,
    w3_ref,
    gain_ref,
    out_ref,
    ctx_k,
    ctx_v,
    logit_out,
    logit_in,
    acc,
    stage,
    landed,
    full,
    new_w,
    fast_ref,
    halo_send,
    halo_recv,
    logit_send,
    logit_recv,
    sum_send,
    sum_recv,
):
    n, heads = shape
    stretches, tokens, width = q_ref.shape
    reach = (WINDOW + tokens - 1) // tokens
    rows = w1_ref.shape[0]
    orders, sizes, halving = plan(n, rows)
    bits = len(sizes)
    me = lax.axis_index("seq")
    my_head = lax.axis_index("head")
    lows = [max(0, o * tokens - WINDOW + 1) // 16 * 16 for o in range(1, reach + 1)]

    for ctx in (ctx_k, ctx_v):
        if lows[-1]:
            ctx[:, : lows[-1], :] = jnp.zeros((stretches, lows[-1], width), ctx.dtype)

        @pl.when(me < reach)
        def _():
            ctx[0, : reach * tokens, :] = jnp.zeros((reach * tokens, width), ctx.dtype)

    barrier = pltpu.get_barrier_semaphore()
    greeted = 0
    for b in range(bits):
        pl.semaphore_signal(
            barrier, inc=1, device_id={"seq": me ^ (1 << b)}, device_id_type=MESH
        )
        greeted += 1
    for o in range(1, reach + 1):
        for d in (o, n - o):
            pl.semaphore_signal(
                barrier, inc=1, device_id={"seq": lax.rem(me + d, n)}, device_id_type=MESH
            )
            greeted += 1
    for p in range(1, heads):
        pl.semaphore_signal(
            barrier, inc=1, device_id={"head": lax.rem(my_head + p, heads)}, device_id_type=MESH
        )
        greeted += 1
    logit_out[...] = jnp.zeros_like(logit_out)
    logit_out[:, : rw_ref.shape[1]] = jnp.dot(
        hid_ref[...], rw_ref[...], preferred_element_type=jnp.float32
    )
    pl.semaphore_wait(barrier, greeted)

    logit_copies = []
    for p in range(1, heads):
        copy = pltpu.make_async_remote_copy(
            src_ref=logit_out,
            dst_ref=logit_in.at[p - 1],
            send_sem=logit_send.at[p - 1],
            recv_sem=logit_recv.at[p - 1],
            device_id={"head": lax.rem(my_head + p, heads)},
            device_id_type=MESH,
        )
        copy.start()
        logit_copies.append(copy)

    def halo_copy(which, o, s, slot):
        source, target = ((k_ref, ctx_k), (v_ref, ctx_v))[which]
        low = lows[o - 1]
        count = tokens - low
        return pltpu.make_async_remote_copy(
            src_ref=source.at[s, pl.ds(low, count), :],
            dst_ref=target.at[slot, pl.ds((reach - o) * tokens + low, count), :],
            send_sem=halo_send.at[which, o - 1, s],
            recv_sem=halo_recv.at[which, o - 1, slot],
            device_id={"seq": lax.rem(me + o, n)},
            device_id_type=MESH,
        )

    def halo_start(o):
        for which in range(2):

            @pl.when(me + o < n)
            def _():
                for s in range(stretches):
                    halo_copy(which, o, s, s).start()

            @pl.when(me + o >= n)
            def _():
                for s in range(stretches - 1):
                    halo_copy(which, o, s, s + 1).start()

    def halo_wait_recv():
        for o in range(1, reach + 1):
            for which in range(2):
                for slot in range(1, stretches):
                    halo_copy(which, o, slot, slot).wait_recv()

                @pl.when(me >= o)
                def _():
                    halo_copy(which, o, 0, 0).wait_recv()

    def halo_wait_send():
        for o in range(1, reach + 1):
            for which in range(2):
                for s in range(stretches - 1):
                    halo_copy(which, o, s, s).wait_send()

                @pl.when(me + o < n)
                def _():
                    halo_copy(which, o, stretches - 1, stretches - 1).wait_send()

    halo_start(1)

    k_now = k_ref[0]
    v_now = v_ref[0]
    gate_pre = contract_last(k_now, w1_ref[...])
    up_pre = contract_last(k_now, w3_ref[...])
    value_back = jnp.dot(v_now, w2_ref[...], preferred_element_type=jnp.float32)
    sigmoid_gate = jax.nn.sigmoid(gate_pre)
    gate_act = gate_pre * sigmoid_gate
    hidden_act = (gate_act * up_pre).astype(jnp.bfloat16)
    for copy in logit_copies:
        copy.wait_recv()
    logits = logit_out[...]
    for p in range(1, heads):
        logits = logits + logit_in[p - 1]
    lane = lax.broadcasted_iota(jnp.int32, logits.shape, 1)

    def rate(j):
        chosen = jnp.sum(jnp.where(lane == 3 * my_head + j, logits, 0.0), axis=1, keepdims=True)
        return jnp.maximum(chosen, 0.0) + jnp.log1p(jnp.exp(-jnp.abs(chosen)))

    base = [0, 0, 0]
    offsets = [sum(sizes[:s]) for s in range(bits)]
    started = {}

    def sum_copy(m, step, source, target, bit):
        copy = pltpu.make_async_remote_copy(
            src_ref=source,
            dst_ref=target,
            send_sem=sum_send.at[m, step],
            recv_sem=sum_recv.at[m, step],
            device_id={"seq": me ^ (1 << bit)},
            device_id_type=MESH,
        )
        copy.start()
        started[m, step] = copy

    def reduce_start(m, step):
        bit, size = orders[m][step], sizes[step]
        if step < halving:
            side = lax.rem(me >> bit, 2)
            give = pl.multiple_of(base[m] + (1 - side) * size, size)
            base[m] = base[m] + side * size
        else:
            give = pl.multiple_of(base[m], size)
            if step > halving:
                started[m, step - 1].wait_send()
        stage[m, pl.ds(give, size), :] = acc[m, pl.ds(give, size), :].astype(stage.dtype)
        sum_copy(
            m, step, stage.at[m, pl.ds(give, size), :], landed.at[m, pl.ds(offsets[step], size), :], bit
        )

    def reduce_end(m, step):
        started[m, step].wait_recv()
        size = sizes[step]
        keep = pl.ds(pl.multiple_of(base[m], size), size)
        acc[m, keep, :] = acc[m, keep, :] + landed[m, pl.ds(offsets[step], size), :].astype(
            jnp.float32
        )

    def gather_start(m, turn):
        bit, size = orders[m][halving - 1 - turn], sizes[halving - 1 - turn]
        part = full.at[m, pl.ds(pl.multiple_of(base[m], size), size), :]
        sum_copy(m, bits + turn, part, part, bit)
        base[m] = base[m] - lax.rem(me >> bit, 2) * size

    scaled_values = (v_now.astype(jnp.float32) * rate(1)).astype(jnp.bfloat16)
    acc[1] = contract_first(scaled_values, hidden_act)
    reduce_start(1, 0)
    up_back = (rate(2) * value_back * gate_act).astype(jnp.bfloat16)
    acc[2] = contract_first(up_back, k_now)
    reduce_start(2, 0)
    gate_back = (
        rate(0) * value_back * up_pre * sigmoid_gate * (1.0 + gate_pre * (1.0 - sigmoid_gate))
    ).astype(jnp.bfloat16)
    acc[0] = contract_first(gate_back, k_now)
    reduce_start(0, 0)
    for o in range(2, reach + 1):
        halo_start(o)

    def fast_apply(inputs, one, two, three):
        gate = contract_last(inputs, one)
        hidden = (gate * jax.nn.sigmoid(gate) * contract_last(inputs, three)).astype(jnp.bfloat16)
        fast = contract_last(hidden, two)
        mean = jnp.mean(fast * fast, axis=-1, keepdims=True)
        return fast * lax.rsqrt(mean + 1e-06) * gain_ref[...]

    fast_ref[0] = fast_apply(q_ref[0], w1_ref[...], w2_ref[...], w3_ref[...])
    ctx_k[:, reach * tokens :, :] = k_ref[...]
    ctx_v[:, reach * tokens :, :] = v_ref[...]

    sequence = (1, 2, 0)
    for step in range(bits):
        for m in sequence:
            reduce_end(m, step)
            if step + 1 < bits:
                reduce_start(m, step + 1)
            else:
                keep = pl.ds(pl.multiple_of(base[m], sizes[-1]), sizes[-1])
                full[m, keep, :] = acc[m, keep, :].astype(full.dtype)
                if halving:
                    gather_start(m, 0)
    for turn in range(1, halving):
        for m in sequence:
            started[m, bits + turn - 1].wait_recv()
            gather_start(m, turn)

    for m in sequence:
        if halving:
            started[m, bits + halving - 1].wait_recv()
        total = full[m].astype(jnp.float32)
        squares = jnp.sum(jnp.sum(total * total, axis=1, keepdims=True), axis=0, keepdims=True)
        new_w[m] = (total * (1.0 / (jnp.sqrt(squares) + norm_floor))).astype(jnp.bfloat16)

        def turn_once(_, carry):
            whole = new_w[m]
            gram = contract_last(whole, whole).astype(jnp.bfloat16)
            product = jnp.dot(gram, whole, preferred_element_type=jnp.float32)
            new_w[m] = (1.5 * whole.astype(jnp.float32) - 0.5 * product).astype(jnp.bfloat16)
            return carry

        lax.fori_loop(0, NS_STEPS, turn_once, 0)
        old = (w1_ref, w2_ref, w3_ref)[m]
        new_w[m] = (
            old[...].astype(jnp.float32) + step_size * new_w[m].astype(jnp.float32)
        ).astype(jnp.bfloat16)
    fast_ref[1] = fast_apply(q_ref[1], new_w[0], new_w[1], new_w[2])

    halo_wait_recv()
    scale = width**-0.5
    span = (reach + 1) * tokens
    query_pos = lax.broadcasted_iota(jnp.int32, (tokens, span), 0)
    key_pos = lax.broadcasted_iota(jnp.int32, (tokens, span), 1) - reach * tokens
    delta = query_pos - key_pos
    for s in range(stretches):
        first = s * n * tokens + me * tokens
        allowed = (delta >= 0) & (delta < WINDOW) & (key_pos + first >= 0)
        scores = jnp.where(allowed, contract_last(q_ref[s], ctx_k[s]) * scale, -1e30)
        expo = jnp.exp(scores - jnp.max(scores, axis=-1, keepdims=True))
        probs = (expo / jnp.sum(expo, axis=-1, keepdims=True)).astype(jnp.bfloat16)
        attended = jnp.dot(probs, ctx_v[s], preferred_element_type=jnp.float32)
        out_ref[s] = (attended + fast_ref[s]).astype(out_ref.dtype)

    halo_wait_send()
    for copy in logit_copies:
        copy.wait_send()
    for (m, step), copy in started.items():
        if not (halving <= step < bits - 1):
            copy.wait_send()


def shards(
    n, heads, queries, key_rows, value_rows, hidden_in, rate_weight, first, down, third, out_gain
):
    stretches, tokens, width = queries.shape
    rows, cols = first.shape[1:]
    reach = (WINDOW + tokens - 1) // tokens
    _, sizes, halving = plan(n, rows)
    bits = len(sizes)
    lanes = -(-rate_weight.shape[1] // 128) * 128
    span = (reach + 1) * tokens
    half, single = jnp.bfloat16, jnp.float32
    peers = max(heads - 1, 1)
    return pl.pallas_call(
        functools.partial(kernel, (n, heads)),
        out_shape=jax.ShapeDtypeStruct(queries.shape, jnp.bfloat16),
        in_specs=[pl.BlockSpec(memory_space=pltpu.VMEM)] * 9,
        out_specs=pl.BlockSpec(memory_space=pltpu.VMEM),
        scratch_shapes=[
            pltpu.VMEM((stretches, span, width), half),
            pltpu.VMEM((stretches, span, width), half),
            pltpu.VMEM((tokens, lanes), single),
            pltpu.VMEM((peers, tokens, lanes), single),
            pltpu.VMEM((3, rows, cols), single),
            pltpu.VMEM((3, rows, cols), half),
            pltpu.VMEM((3, max(sum(sizes), 16), cols), half),
            pltpu.VMEM((3, rows, cols), half),
            pltpu.VMEM((3, rows, cols), half),
            pltpu.VMEM((stretches, tokens, width), single),
            pltpu.SemaphoreType.DMA((2, reach, stretches)),
            pltpu.SemaphoreType.DMA((2, reach, stretches)),
            pltpu.SemaphoreType.DMA((peers,)),
            pltpu.SemaphoreType.DMA((peers,)),
            pltpu.SemaphoreType.DMA((3, bits + halving)),
            pltpu.SemaphoreType.DMA((3, bits + halving)),
        ],
        compiler_params=pltpu.CompilerParams(
            collective_id=0, has_side_effects=True, vmem_limit_bytes=40 * 1024 * 1024
        ),
    )(
        queries,
        key_rows,
        value_rows,
        hidden_in,
        rate_weight,
        first[0],
        down[0],
        third[0],
        out_gain.reshape(1, -1),
    )


def solution(mesh):
    return jax.shard_map(
        functools.partial(shards, mesh.shape["seq"], mesh.shape["head"]),
        mesh=mesh,
        in_specs=(
            P(None, "seq", "head"),
            P(None, "seq", "head"),
            P(None, "seq", "head"),
            P("seq", "head"),
            P("head", None),
            P("head", None, None),
            P("head", None, None),
            P("head", None, None),
            P("head"),
        ),
        out_specs=P(None, "seq", "head"),
        check_vma=False,
    )
```

```python
import functools

import jax
import jax.numpy as jnp
from jax import lax
from jax.experimental import pallas as pl
from jax.experimental.pallas import tpu as pltpu
from jax.sharding import PartitionSpec as P

WINDOW = 512
NS_STEPS = 3
LEAST_ROWS = 64
RELAYS = (0, 0, 0, 2)
MESH = pl.DeviceIdType.MESH

step_size = 1.0
norm_floor = 1e-07


def contract_last(left, right):
    return lax.dot_general(
        left, right, (((1,), (1,)), ((), ())), preferred_element_type=jnp.float32
    )


def contract_first(left, right):
    return lax.dot_general(
        left, right, (((0,), (0,)), ((), ())), preferred_element_type=jnp.float32
    )


def plan(seq_count, rows):
    bits = seq_count.bit_length() - 1
    turning = min(3, bits)
    orders = []
    for m in range(3):
        first = [(m + s) % turning for s in range(turning)] if turning else []
        orders.append(first + list(range(turning, bits)))
    sizes, held, halving = [], rows, 0
    for _ in range(bits):
        if held // 2 >= LEAST_ROWS:
            held //= 2
            halving += 1
        sizes.append(held)
    return orders, sizes, halving


def kernel(
    shape,
    q_hbm,
    k_ref,
    v_ref,
    hid_hbm,
    rw_hbm,
    w1_hbm,
    w2_hbm,
    w3_hbm,
    gain_hbm,
    out_ref,
    q_ref,
    hid_ref,
    rw_ref,
    w1_ref,
    w2_ref,
    w3_ref,
    gain_ref,
    ctx_k,
    ctx_v,
    logit_out,
    logit_in,
    acc,
    stage,
    landed,
    full,
    new_w,
    fast_ref,
    halo_send,
    halo_recv,
    logit_send,
    logit_recv,
    sum_send,
    sum_recv,
    relay_send,
    local_sem,
):
    n, heads = shape
    stretches, tokens, width = q_ref.shape
    reach = (WINDOW + tokens - 1) // tokens
    rows = w1_ref.shape[0]
    own = pl.ds(reach * tokens, tokens)
    moves = {}
    for index, (name, source, target) in enumerate((
        ("hid", hid_hbm, hid_ref),
        ("rw", rw_hbm, rw_ref),
        ("k", k_ref, ctx_k.at[:, own, :]),
        ("w1", w1_hbm.at[0], w1_ref),
        ("w3", w3_hbm.at[0], w3_ref),
        ("v", v_ref, ctx_v.at[:, own, :]),
        ("w2", w2_hbm.at[0], w2_ref),
        ("q", q_hbm, q_ref),
        ("gain", gain_hbm, gain_ref),
    )):
        moves[name] = pltpu.make_async_copy(source, target, local_sem.at[index])
        moves[name].start()
    orders, sizes, halving = plan(n, rows)
    bits = len(sizes)
    me = lax.axis_index("seq")
    my_head = lax.axis_index("head")
    lows = [max(0, o * tokens - WINDOW + 1) // 16 * 16 for o in range(1, reach + 1)]

    for ctx in (ctx_k, ctx_v):
        if lows[-1]:
            ctx[:, : lows[-1], :] = jnp.zeros((stretches, lows[-1], width), ctx.dtype)

        @pl.when(me < reach)
        def _():
            ctx[0, : reach * tokens, :] = jnp.zeros((reach * tokens, width), ctx.dtype)

    barrier = pltpu.get_barrier_semaphore()
    greeted = 0
    for b in range(bits):
        pl.semaphore_signal(
            barrier, inc=1, device_id={"seq": me ^ (1 << b)}, device_id_type=MESH
        )
        greeted += 1
    for o in range(1, reach + 1):
        for d in (o, n - o):
            pl.semaphore_signal(
                barrier, inc=1, device_id={"seq": lax.rem(me + d, n)}, device_id_type=MESH
            )
            greeted += 1
    for p in range(1, heads):
        pl.semaphore_signal(
            barrier, inc=1, device_id={"head": lax.rem(my_head + p, heads)}, device_id_type=MESH
        )
        greeted += 1
    logit_out[...] = jnp.zeros_like(logit_out)
    moves["hid"].wait()
    moves["rw"].wait()
    logit_out[:, : rw_ref.shape[0]] = contract_last(hid_ref[...], rw_ref[...])
    pl.semaphore_wait(barrier, greeted)

    logit_copies = []
    for p in range(1, heads):
        copy = pltpu.make_async_remote_copy(
            src_ref=logit_out,
            dst_ref=logit_in.at[p - 1],
            send_sem=logit_send.at[p - 1],
            recv_sem=logit_recv.at[p - 1],
            device_id={"head": lax.rem(my_head + p, heads)},
            device_id_type=MESH,
        )
        copy.start()
        logit_copies.append(copy)

    def halo_copy(which, o, s, slot):
        source, target = ((k_ref, ctx_k), (v_ref, ctx_v))[which]
        low = lows[o - 1]
        count = tokens - low
        return pltpu.make_async_remote_copy(
            src_ref=source.at[s, pl.ds(low, count), :],
            dst_ref=target.at[slot, pl.ds((reach - o) * tokens + low, count), :],
            send_sem=halo_send.at[which, o - 1, s],
            recv_sem=halo_recv.at[which, o - 1, slot],
            device_id={"seq": lax.rem(me + o, n)},
            device_id_type=MESH,
        )

    relayed = reach == 3 and n % 2 == 0
    odd = lax.rem(me, 2)

    def halo_start(o):
        sends = (odd == (1 if o == 3 else 0)) if relayed and o != 2 else (odd >= 0)
        for s in range(stretches):
            for which in range(2):

                @pl.when(sends & (me + o < n))
                def _():
                    halo_copy(which, o, s, s).start()

                if s + 1 < stretches:

                    @pl.when(sends & (me + o >= n))
                    def _():
                        halo_copy(which, o, s, s + 1).start()

    def relay_copy(which, slot, onward):
        target = (ctx_k, ctx_v)[which]
        o, low = (3, lows[2]) if onward else (1, 0)
        count = tokens - low
        return pltpu.make_async_remote_copy(
            src_ref=target.at[slot, pl.ds((reach - 2) * tokens + low, count), :],
            dst_ref=target.at[slot, pl.ds((reach - o) * tokens + low, count), :],
            send_sem=relay_send.at[which, slot],
            recv_sem=halo_recv.at[which, o - 1, slot],
            device_id={"seq": me + 1 if onward else me - 1},
            device_id_type=MESH,
        )

    def each_relay(which, slot, act):
        for onward in (True, False):
            ready = odd == (0 if onward else 1)
            if slot == 0:
                ready = ready & (me >= 2)

            @pl.when(ready)
            def _():
                act(relay_copy(which, slot, onward))

    def wait_block(which, o, slot):
        if slot == 0:

            @pl.when(me >= o)
            def _():
                halo_copy(which, o, 0, 0).wait_recv()

        else:
            halo_copy(which, o, slot, slot).wait_recv()

    def relay(which, slot):
        wait_block(which, 2, slot)
        each_relay(which, slot, lambda copy: copy.start())

    def halo_wait_recv(chosen):
        for slot in range(stretches):
            for which in range(2):
                for o in chosen:
                    wait_block(which, o, slot)

    def halo_wait_send():
        for o in range(1, reach + 1):
            sends = (odd == (1 if o == 3 else 0)) if relayed and o != 2 else (odd >= 0)
            for which in range(2):
                for s in range(stretches):
                    goes = sends if s + 1 < stretches else sends & (me + o < n)

                    @pl.when(goes)
                    def _():
                        halo_copy(which, o, s, s).wait_send()

        if relayed:
            for which in range(2):
                for slot in range(stretches):
                    each_relay(which, slot, lambda copy: copy.wait_send())

    relays = [(which, slot) for slot in range(stretches) for which in range(2)] if relayed else []

    def relay_next(count):
        for _ in range(min(count, len(relays))):
            relay(*relays.pop(0))

    order = [2, 1, 3] if relayed else list(range(1, reach + 1))
    for o in order[:2]:
        halo_start(o)

    moves["k"].wait()
    moves["w1"].wait()
    moves["w3"].wait()
    k_now = ctx_k[0, reach * tokens :, :]
    gate_pre = contract_last(k_now, w1_ref[...])
    up_pre = contract_last(k_now, w3_ref[...])
    moves["v"].wait()
    moves["w2"].wait()
    v_now = ctx_v[0, reach * tokens :, :]
    value_back = jnp.dot(v_now, w2_ref[...], preferred_element_type=jnp.float32)
    sigmoid_gate = jax.nn.sigmoid(gate_pre)
    gate_act = gate_pre * sigmoid_gate
    hidden_act = (gate_act * up_pre).astype(jnp.bfloat16)
    for copy in logit_copies:
        copy.wait_recv()
    logits = logit_out[...]
    for p in range(1, heads):
        logits = logits + logit_in[p - 1]
    lane = lax.broadcasted_iota(jnp.int32, logits.shape, 1)

    def rate(j):
        chosen = jnp.sum(jnp.where(lane == 3 * my_head + j, logits, 0.0), axis=1, keepdims=True)
        return jnp.maximum(chosen, 0.0) + jnp.log1p(jnp.exp(-jnp.abs(chosen)))

    base = [0, 0, 0]
    offsets = [sum(sizes[:s]) for s in range(bits)]
    started = {}

    def sum_copy(m, step, source, target, bit):
        copy = pltpu.make_async_remote_copy(
            src_ref=source,
            dst_ref=target,
            send_sem=sum_send.at[m, step],
            recv_sem=sum_recv.at[m, step],
            device_id={"seq": me ^ (1 << bit)},
            device_id_type=MESH,
        )
        copy.start()
        started[m, step] = copy

    def reduce_start(m, step):
        bit, size = orders[m][step], sizes[step]
        if step < halving:
            side = lax.rem(me >> bit, 2)
            give = pl.multiple_of(base[m] + (1 - side) * size, size)
            base[m] = base[m] + side * size
        else:
            give = pl.multiple_of(base[m], size)
            if step > halving:
                started[m, step - 1].wait_send()
        stage[m, pl.ds(give, size), :] = acc[m, pl.ds(give, size), :].astype(stage.dtype)
        sum_copy(
            m, step, stage.at[m, pl.ds(give, size), :], landed.at[m, pl.ds(offsets[step], size), :], bit
        )

    def reduce_end(m, step):
        started[m, step].wait_recv()
        size = sizes[step]
        keep = pl.ds(pl.multiple_of(base[m], size), size)
        acc[m, keep, :] = acc[m, keep, :] + landed[m, pl.ds(offsets[step], size), :].astype(
            jnp.float32
        )

    def gather_start(m, turn):
        bit, size = orders[m][halving - 1 - turn], sizes[halving - 1 - turn]
        part = full.at[m, pl.ds(pl.multiple_of(base[m], size), size), :]
        sum_copy(m, bits + turn, part, part, bit)
        base[m] = base[m] - lax.rem(me >> bit, 2) * size

    scaled_values = (v_now.astype(jnp.float32) * rate(1)).astype(jnp.bfloat16)
    acc[1] = contract_first(scaled_values, hidden_act)
    reduce_start(1, 0)
    up_back = (rate(2) * value_back * gate_act).astype(jnp.bfloat16)
    acc[2] = contract_first(up_back, k_now)
    reduce_start(2, 0)
    gate_back = (
        rate(0) * value_back * up_pre * sigmoid_gate * (1.0 + gate_pre * (1.0 - sigmoid_gate))
    ).astype(jnp.bfloat16)
    acc[0] = contract_first(gate_back, k_now)
    reduce_start(0, 0)
    for o in order[2:]:
        halo_start(o)

    def fast_apply(inputs, one, two, three):
        gate = contract_last(inputs, one)
        hidden = (gate * jax.nn.sigmoid(gate) * contract_last(inputs, three)).astype(jnp.bfloat16)
        fast = contract_last(hidden, two)
        mean = jnp.mean(fast * fast, axis=-1, keepdims=True)
        return fast * lax.rsqrt(mean + 1e-06) * gain_ref[...]

    moves["q"].wait()
    moves["gain"].wait()
    fast_ref[0] = fast_apply(q_ref[0], w1_ref[...], w2_ref[...], w3_ref[...])

    sequence = (1, 2, 0)
    for step in range(bits):
        relay_next(RELAYS[min(step, len(RELAYS) - 1)])
        for m in sequence:
            reduce_end(m, step)
            if step + 1 < bits:
                reduce_start(m, step + 1)
            else:
                keep = pl.ds(pl.multiple_of(base[m], sizes[-1]), sizes[-1])
                full[m, keep, :] = acc[m, keep, :].astype(full.dtype)
                if halving:
                    gather_start(m, 0)
    relay_next(len(relays))
    for turn in range(1, halving):
        for m in sequence:
            started[m, bits + turn - 1].wait_recv()
            gather_start(m, turn)

    for m in sequence:
        if halving:
            started[m, bits + halving - 1].wait_recv()
        total = full[m].astype(jnp.float32)
        squares = jnp.sum(jnp.sum(total * total, axis=1, keepdims=True), axis=0, keepdims=True)
        new_w[m] = (total * (1.0 / (jnp.sqrt(squares) + norm_floor))).astype(jnp.bfloat16)

        def turn_once(_, carry):
            whole = new_w[m]
            gram = contract_last(whole, whole).astype(jnp.bfloat16)
            product = jnp.dot(gram, whole, preferred_element_type=jnp.float32)
            new_w[m] = (1.5 * whole.astype(jnp.float32) - 0.5 * product).astype(jnp.bfloat16)
            return carry

        lax.fori_loop(0, NS_STEPS, turn_once, 0)
        old = (w1_ref, w2_ref, w3_ref)[m]
        new_w[m] = (
            old[...].astype(jnp.float32) + step_size * new_w[m].astype(jnp.float32)
        ).astype(jnp.bfloat16)
    fast_ref[1] = fast_apply(q_ref[1], new_w[0], new_w[1], new_w[2])

    halo_wait_recv([o for o in range(1, reach + 1) if not (relayed and o == 2)])
    scale = width**-0.5
    span = (reach + 1) * tokens
    query_pos = lax.broadcasted_iota(jnp.int32, (tokens, span), 0)
    key_pos = lax.broadcasted_iota(jnp.int32, (tokens, span), 1) - reach * tokens
    delta = query_pos - key_pos
    for s in range(stretches):
        first = s * n * tokens + me * tokens
        allowed = (delta >= 0) & (delta < WINDOW) & (key_pos + first >= 0)
        scores = jnp.where(allowed, contract_last(q_ref[s], ctx_k[s]) * scale, -1e30)
        expo = jnp.exp(scores - jnp.max(scores, axis=-1, keepdims=True))
        probs = (expo / jnp.sum(expo, axis=-1, keepdims=True)).astype(jnp.bfloat16)
        attended = jnp.dot(probs, ctx_v[s], preferred_element_type=jnp.float32)
        out_ref[s] = (attended + fast_ref[s]).astype(out_ref.dtype)

    halo_wait_send()
    for copy in logit_copies:
        copy.wait_send()
    for (m, step), copy in started.items():
        if not (halving <= step < bits - 1):
            copy.wait_send()


def shards(
    n, heads, queries, key_rows, value_rows, hidden_in, rate_weight, first, down, third, out_gain
):
    stretches, tokens, width = queries.shape
    rows, cols = first.shape[1:]
    reach = (WINDOW + tokens - 1) // tokens
    _, sizes, halving = plan(n, rows)
    bits = len(sizes)
    lanes = -(-rate_weight.shape[1] // 128) * 128
    span = (reach + 1) * tokens
    half, single = jnp.bfloat16, jnp.float32
    peers = max(heads - 1, 1)
    return pl.pallas_call(
        functools.partial(kernel, (n, heads)),
        out_shape=jax.ShapeDtypeStruct(queries.shape, jnp.bfloat16),
        in_specs=[pl.BlockSpec(memory_space=pltpu.HBM)] * 9,
        out_specs=pl.BlockSpec(memory_space=pltpu.VMEM),
        scratch_shapes=[
            pltpu.VMEM(queries.shape, half),
            pltpu.VMEM(hidden_in.shape, half),
            pltpu.VMEM(rate_weight.shape[::-1], half),
            pltpu.VMEM((rows, cols), half),
            pltpu.VMEM((rows, cols), half),
            pltpu.VMEM((rows, cols), half),
            pltpu.VMEM((1, width), single),
            pltpu.VMEM((stretches, span, width), half),
            pltpu.VMEM((stretches, span, width), half),
            pltpu.VMEM((tokens, lanes), single),
            pltpu.VMEM((peers, tokens, lanes), single),
            pltpu.VMEM((3, rows, cols), single),
            pltpu.VMEM((3, rows, cols), half),
            pltpu.VMEM((3, max(sum(sizes), 16), cols), half),
            pltpu.VMEM((3, rows, cols), half),
            pltpu.VMEM((3, rows, cols), half),
            pltpu.VMEM((stretches, tokens, width), single),
            pltpu.SemaphoreType.DMA((2, reach, stretches)),
            pltpu.SemaphoreType.DMA((2, reach, stretches)),
            pltpu.SemaphoreType.DMA((peers,)),
            pltpu.SemaphoreType.DMA((peers,)),
            pltpu.SemaphoreType.DMA((3, bits + halving)),
            pltpu.SemaphoreType.DMA((3, bits + halving)),
            pltpu.SemaphoreType.DMA((2, stretches)),
            pltpu.SemaphoreType.DMA((9,)),
        ],
        compiler_params=pltpu.CompilerParams(
            collective_id=0, has_side_effects=True, vmem_limit_bytes=60 * 1024 * 1024
        ),
    )(
        queries,
        key_rows,
        value_rows,
        hidden_in,
        rate_weight.T,
        first,
        down,
        third,
        out_gain.reshape(1, -1),
    )


def solution(mesh):
    return jax.shard_map(
        functools.partial(shards, mesh.shape["seq"], mesh.shape["head"]),
        mesh=mesh,
        in_specs=(
            P(None, "seq", "head"),
            P(None, "seq", "head"),
            P(None, "seq", "head"),
            P("seq", "head"),
            P("head", None),
            P("head", None, None),
            P("head", None, None),
            P("head", None, None),
            P("head"),
        ),
        out_specs=P(None, "seq", "head"),
        check_vma=False,
    )
```

```python
import functools

import jax
import jax.numpy as jnp
from jax import lax
from jax.experimental import pallas as pl
from jax.experimental.pallas import tpu as pltpu
from jax.sharding import PartitionSpec as P

WINDOW = 512
NS_STEPS = 3
LEAST_ROWS = 64
RELAYS = (0, 0, 0, 2)
MESH = pl.DeviceIdType.MESH

step_size = 1.0
norm_floor = 1e-07


def contract_last(left, right):
    return lax.dot_general(
        left, right, (((1,), (1,)), ((), ())), preferred_element_type=jnp.float32
    )


def contract_first(left, right):
    return lax.dot_general(
        left, right, (((0,), (0,)), ((), ())), preferred_element_type=jnp.float32
    )


def plan(seq_count, rows):
    bits = seq_count.bit_length() - 1
    turning = min(3, bits)
    orders = []
    for m in range(3):
        first = [(m + s) % turning for s in range(turning)] if turning else []
        orders.append(first + list(range(turning, bits)))
    sizes, held, halving = [], rows, 0
    for _ in range(bits):
        if held // 2 >= LEAST_ROWS:
            held //= 2
            halving += 1
        sizes.append(held)
    return orders, sizes, halving


def kernel(
    shape,
    q_hbm,
    k_ref,
    v_ref,
    hid_hbm,
    rw_hbm,
    w1_hbm,
    w2_hbm,
    w3_hbm,
    gain_hbm,
    out_ref,
    q_ref,
    hid_ref,
    rw_ref,
    w1_ref,
    w2_ref,
    w3_ref,
    gain_ref,
    ctx_k,
    ctx_v,
    logit_out,
    logit_in,
    acc,
    stage,
    landed,
    full,
    new_w,
    fast_ref,
    attended_ref,
    halo_send,
    halo_recv,
    logit_send,
    logit_recv,
    sum_send,
    sum_recv,
    relay_send,
    local_sem,
):
    n, heads = shape
    stretches, tokens, width = q_ref.shape
    reach = (WINDOW + tokens - 1) // tokens
    rows = w1_ref.shape[0]
    own = pl.ds(reach * tokens, tokens)
    moves = {}
    for index, (name, source, target) in enumerate((
        ("hid", hid_hbm, hid_ref),
        ("rw", rw_hbm, rw_ref),
        ("k", k_ref, ctx_k.at[:, own, :]),
        ("w1", w1_hbm.at[0], w1_ref),
        ("w3", w3_hbm.at[0], w3_ref),
        ("v", v_ref, ctx_v.at[:, own, :]),
        ("w2", w2_hbm.at[0], w2_ref),
        ("q", q_hbm, q_ref),
        ("gain", gain_hbm, gain_ref),
    )):
        moves[name] = pltpu.make_async_copy(source, target, local_sem.at[index])
        moves[name].start()
    orders, sizes, halving = plan(n, rows)
    bits = len(sizes)
    me = lax.axis_index("seq")
    my_head = lax.axis_index("head")
    lows = [max(0, o * tokens - WINDOW + 1) // 16 * 16 for o in range(1, reach + 1)]

    for ctx in (ctx_k, ctx_v):
        if lows[-1]:
            ctx[:, : lows[-1], :] = jnp.zeros((stretches, lows[-1], width), ctx.dtype)

        @pl.when(me < reach)
        def _():
            ctx[0, : reach * tokens, :] = jnp.zeros((reach * tokens, width), ctx.dtype)

    barrier = pltpu.get_barrier_semaphore()
    greeted = 0
    for b in range(bits):
        pl.semaphore_signal(
            barrier, inc=1, device_id={"seq": me ^ (1 << b)}, device_id_type=MESH
        )
        greeted += 1
    for o in range(1, reach + 1):
        for d in (o, n - o):
            pl.semaphore_signal(
                barrier, inc=1, device_id={"seq": lax.rem(me + d, n)}, device_id_type=MESH
            )
            greeted += 1
    for p in range(1, heads):
        pl.semaphore_signal(
            barrier, inc=1, device_id={"head": lax.rem(my_head + p, heads)}, device_id_type=MESH
        )
        greeted += 1
    logit_out[...] = jnp.zeros_like(logit_out)
    moves["hid"].wait()
    moves["rw"].wait()
    logit_out[:, : rw_ref.shape[0]] = contract_last(hid_ref[...], rw_ref[...])
    pl.semaphore_wait(barrier, greeted)

    logit_copies = []
    for p in range(1, heads):
        copy = pltpu.make_async_remote_copy(
            src_ref=logit_out,
            dst_ref=logit_in.at[p - 1],
            send_sem=logit_send.at[p - 1],
            recv_sem=logit_recv.at[p - 1],
            device_id={"head": lax.rem(my_head + p, heads)},
            device_id_type=MESH,
        )
        copy.start()
        logit_copies.append(copy)

    def halo_copy(which, o, s, slot):
        source, target = ((k_ref, ctx_k), (v_ref, ctx_v))[which]
        low = lows[o - 1]
        count = tokens - low
        return pltpu.make_async_remote_copy(
            src_ref=source.at[s, pl.ds(low, count), :],
            dst_ref=target.at[slot, pl.ds((reach - o) * tokens + low, count), :],
            send_sem=halo_send.at[which, o - 1, s],
            recv_sem=halo_recv.at[which, o - 1, slot],
            device_id={"seq": lax.rem(me + o, n)},
            device_id_type=MESH,
        )

    relayed = reach == 3 and n % 2 == 0
    odd = lax.rem(me, 2)

    def halo_start(o):
        sends = (odd == (1 if o == 3 else 0)) if relayed and o != 2 else (odd >= 0)
        for s in range(stretches):
            for which in range(2):

                @pl.when(sends & (me + o < n))
                def _():
                    halo_copy(which, o, s, s).start()

                if s + 1 < stretches:

                    @pl.when(sends & (me + o >= n))
                    def _():
                        halo_copy(which, o, s, s + 1).start()

    def relay_copy(which, slot, onward):
        target = (ctx_k, ctx_v)[which]
        o, low = (3, lows[2]) if onward else (1, 0)
        count = tokens - low
        return pltpu.make_async_remote_copy(
            src_ref=target.at[slot, pl.ds((reach - 2) * tokens + low, count), :],
            dst_ref=target.at[slot, pl.ds((reach - o) * tokens + low, count), :],
            send_sem=relay_send.at[which, slot],
            recv_sem=halo_recv.at[which, o - 1, slot],
            device_id={"seq": me + 1 if onward else me - 1},
            device_id_type=MESH,
        )

    def each_relay(which, slot, act):
        for onward in (True, False):
            ready = odd == (0 if onward else 1)
            if slot == 0:
                ready = ready & (me >= 2)

            @pl.when(ready)
            def _():
                act(relay_copy(which, slot, onward))

    def wait_block(which, o, slot):
        if slot == 0:

            @pl.when(me >= o)
            def _():
                halo_copy(which, o, 0, 0).wait_recv()

        else:
            halo_copy(which, o, slot, slot).wait_recv()

    def relay(which, slot):
        wait_block(which, 2, slot)
        each_relay(which, slot, lambda copy: copy.start())

    def halo_wait_recv(chosen):
        for slot in range(stretches):
            for which in range(2):
                for o in chosen:
                    wait_block(which, o, slot)

    def halo_wait_send():
        for o in range(1, reach + 1):
            sends = (odd == (1 if o == 3 else 0)) if relayed and o != 2 else (odd >= 0)
            for which in range(2):
                for s in range(stretches):
                    goes = sends if s + 1 < stretches else sends & (me + o < n)

                    @pl.when(goes)
                    def _():
                        halo_copy(which, o, s, s).wait_send()

        if relayed:
            for which in range(2):
                for slot in range(stretches):
                    each_relay(which, slot, lambda copy: copy.wait_send())

    relays = [(which, slot) for slot in range(stretches) for which in range(2)] if relayed else []

    def relay_next(count):
        for _ in range(min(count, len(relays))):
            relay(*relays.pop(0))

    order = [2, 1, 3] if relayed else list(range(1, reach + 1))
    for o in order[:2]:
        halo_start(o)

    moves["k"].wait()
    moves["w1"].wait()
    moves["w3"].wait()
    k_now = ctx_k[0, reach * tokens :, :]
    gate_pre = contract_last(k_now, w1_ref[...])
    up_pre = contract_last(k_now, w3_ref[...])
    moves["v"].wait()
    moves["w2"].wait()
    v_now = ctx_v[0, reach * tokens :, :]
    value_back = jnp.dot(v_now, w2_ref[...], preferred_element_type=jnp.float32)
    sigmoid_gate = jax.nn.sigmoid(gate_pre)
    gate_act = gate_pre * sigmoid_gate
    hidden_act = (gate_act * up_pre).astype(jnp.bfloat16)
    for copy in logit_copies:
        copy.wait_recv()
    logits = logit_out[...]
    for p in range(1, heads):
        logits = logits + logit_in[p - 1]
    lane = lax.broadcasted_iota(jnp.int32, logits.shape, 1)

    def rate(j):
        chosen = jnp.sum(jnp.where(lane == 3 * my_head + j, logits, 0.0), axis=1, keepdims=True)
        return jnp.maximum(chosen, 0.0) + jnp.log1p(jnp.exp(-jnp.abs(chosen)))

    base = [0, 0, 0]
    offsets = [sum(sizes[:s]) for s in range(bits)]
    started = {}

    def sum_copy(m, step, source, target, bit):
        copy = pltpu.make_async_remote_copy(
            src_ref=source,
            dst_ref=target,
            send_sem=sum_send.at[m, step],
            recv_sem=sum_recv.at[m, step],
            device_id={"seq": me ^ (1 << bit)},
            device_id_type=MESH,
        )
        copy.start()
        started[m, step] = copy

    def reduce_start(m, step):
        bit, size = orders[m][step], sizes[step]
        if step < halving:
            side = lax.rem(me >> bit, 2)
            give = pl.multiple_of(base[m] + (1 - side) * size, size)
            base[m] = base[m] + side * size
        else:
            give = pl.multiple_of(base[m], size)
            if step > halving:
                started[m, step - 1].wait_send()
        stage[m, pl.ds(give, size), :] = acc[m, pl.ds(give, size), :].astype(stage.dtype)
        sum_copy(
            m, step, stage.at[m, pl.ds(give, size), :], landed.at[m, pl.ds(offsets[step], size), :], bit
        )

    def reduce_end(m, step):
        started[m, step].wait_recv()
        size = sizes[step]
        keep = pl.ds(pl.multiple_of(base[m], size), size)
        acc[m, keep, :] = acc[m, keep, :] + landed[m, pl.ds(offsets[step], size), :].astype(
            jnp.float32
        )

    def gather_start(m, turn):
        bit, size = orders[m][halving - 1 - turn], sizes[halving - 1 - turn]
        part = full.at[m, pl.ds(pl.multiple_of(base[m], size), size), :]
        sum_copy(m, bits + turn, part, part, bit)
        base[m] = base[m] - lax.rem(me >> bit, 2) * size

    scaled_values = (v_now.astype(jnp.float32) * rate(1)).astype(jnp.bfloat16)
    acc[1] = contract_first(scaled_values, hidden_act)
    reduce_start(1, 0)
    up_back = (rate(2) * value_back * gate_act).astype(jnp.bfloat16)
    acc[2] = contract_first(up_back, k_now)
    reduce_start(2, 0)
    gate_back = (
        rate(0) * value_back * up_pre * sigmoid_gate * (1.0 + gate_pre * (1.0 - sigmoid_gate))
    ).astype(jnp.bfloat16)
    acc[0] = contract_first(gate_back, k_now)
    reduce_start(0, 0)
    for o in order[2:]:
        halo_start(o)

    def fast_apply(inputs, one, two, three):
        gate = contract_last(inputs, one)
        hidden = (gate * jax.nn.sigmoid(gate) * contract_last(inputs, three)).astype(jnp.bfloat16)
        fast = contract_last(hidden, two)
        mean = jnp.mean(fast * fast, axis=-1, keepdims=True)
        return fast * lax.rsqrt(mean + 1e-06) * gain_ref[...]

    moves["q"].wait()
    moves["gain"].wait()
    fast_ref[0] = fast_apply(q_ref[0], w1_ref[...], w2_ref[...], w3_ref[...])

    sequence = (1, 2, 0)
    for step in range(bits):
        relay_next(RELAYS[min(step, len(RELAYS) - 1)])
        for m in sequence:
            reduce_end(m, step)
            if step + 1 < bits:
                reduce_start(m, step + 1)
            else:
                keep = pl.ds(pl.multiple_of(base[m], sizes[-1]), sizes[-1])
                full[m, keep, :] = acc[m, keep, :].astype(full.dtype)
                if halving:
                    gather_start(m, 0)
    relay_next(len(relays))
    for turn in range(1, halving):
        for m in sequence:
            started[m, bits + turn - 1].wait_recv()
            gather_start(m, turn)

    halo_wait_recv([o for o in range(1, reach + 1) if not (relayed and o == 2)])
    scale = width**-0.5
    span = (reach + 1) * tokens
    query_pos = lax.broadcasted_iota(jnp.int32, (tokens, span), 0)
    key_pos = lax.broadcasted_iota(jnp.int32, (tokens, span), 1) - reach * tokens
    delta = query_pos - key_pos
    for s in range(stretches):
        first = s * n * tokens + me * tokens
        allowed = (delta >= 0) & (delta < WINDOW) & (key_pos + first >= 0)
        scores = jnp.where(allowed, contract_last(q_ref[s], ctx_k[s]) * scale, -1e30)
        expo = jnp.exp(scores - jnp.max(scores, axis=-1, keepdims=True))
        probs = (expo / jnp.sum(expo, axis=-1, keepdims=True)).astype(jnp.bfloat16)
        attended = jnp.dot(probs, ctx_v[s], preferred_element_type=jnp.float32)
        attended_ref[s] = attended

    for m in sequence:
        if halving:
            started[m, bits + halving - 1].wait_recv()
        total = full[m].astype(jnp.float32)
        squares = jnp.sum(jnp.sum(total * total, axis=1, keepdims=True), axis=0, keepdims=True)
        new_w[m] = (total * (1.0 / (jnp.sqrt(squares) + norm_floor))).astype(jnp.bfloat16)

        def turn_once(_, carry):
            whole = new_w[m]
            gram = contract_last(whole, whole).astype(jnp.bfloat16)
            product = jnp.dot(gram, whole, preferred_element_type=jnp.float32)
            new_w[m] = (1.5 * whole.astype(jnp.float32) - 0.5 * product).astype(jnp.bfloat16)
            return carry

        lax.fori_loop(0, NS_STEPS, turn_once, 0)
        old = (w1_ref, w2_ref, w3_ref)[m]
        new_w[m] = (
            old[...].astype(jnp.float32) + step_size * new_w[m].astype(jnp.float32)
        ).astype(jnp.bfloat16)
    out_ref[0] = (attended_ref[0] + fast_ref[0]).astype(out_ref.dtype)
    late = fast_apply(q_ref[1], new_w[0], new_w[1], new_w[2])
    out_ref[1] = (attended_ref[1] + late).astype(out_ref.dtype)

    halo_wait_send()
    for copy in logit_copies:
        copy.wait_send()
    for (m, step), copy in started.items():
        if not (halving <= step < bits - 1):
            copy.wait_send()


def shards(
    n, heads, queries, key_rows, value_rows, hidden_in, rate_weight, first, down, third, out_gain
):
    stretches, tokens, width = queries.shape
    rows, cols = first.shape[1:]
    reach = (WINDOW + tokens - 1) // tokens
    _, sizes, halving = plan(n, rows)
    bits = len(sizes)
    lanes = -(-rate_weight.shape[1] // 128) * 128
    span = (reach + 1) * tokens
    half, single = jnp.bfloat16, jnp.float32
    peers = max(heads - 1, 1)
    return pl.pallas_call(
        functools.partial(kernel, (n, heads)),
        out_shape=jax.ShapeDtypeStruct(queries.shape, jnp.bfloat16),
        in_specs=[pl.BlockSpec(memory_space=pltpu.HBM)] * 9,
        out_specs=pl.BlockSpec(memory_space=pltpu.VMEM),
        scratch_shapes=[
            pltpu.VMEM(queries.shape, half),
            pltpu.VMEM(hidden_in.shape, half),
            pltpu.VMEM(rate_weight.shape[::-1], half),
            pltpu.VMEM((rows, cols), half),
            pltpu.VMEM((rows, cols), half),
            pltpu.VMEM((rows, cols), half),
            pltpu.VMEM((1, width), single),
            pltpu.VMEM((stretches, span, width), half),
            pltpu.VMEM((stretches, span, width), half),
            pltpu.VMEM((tokens, lanes), single),
            pltpu.VMEM((peers, tokens, lanes), single),
            pltpu.VMEM((3, rows, cols), single),
            pltpu.VMEM((3, rows, cols), half),
            pltpu.VMEM((3, max(sum(sizes), 16), cols), half),
            pltpu.VMEM((3, rows, cols), half),
            pltpu.VMEM((3, rows, cols), half),
            pltpu.VMEM((stretches, tokens, width), single),
            pltpu.VMEM((stretches, tokens, width), single),
            pltpu.SemaphoreType.DMA((2, reach, stretches)),
            pltpu.SemaphoreType.DMA((2, reach, stretches)),
            pltpu.SemaphoreType.DMA((peers,)),
            pltpu.SemaphoreType.DMA((peers,)),
            pltpu.SemaphoreType.DMA((3, bits + halving)),
            pltpu.SemaphoreType.DMA((3, bits + halving)),
            pltpu.SemaphoreType.DMA((2, stretches)),
            pltpu.SemaphoreType.DMA((9,)),
        ],
        compiler_params=pltpu.CompilerParams(
            collective_id=0, has_side_effects=True, vmem_limit_bytes=60 * 1024 * 1024
        ),
    )(
        queries,
        key_rows,
        value_rows,
        hidden_in,
        rate_weight.T,
        first,
        down,
        third,
        out_gain.reshape(1, -1),
    )


def solution(mesh):
    return jax.shard_map(
        functools.partial(shards, mesh.shape["seq"], mesh.shape["head"]),
        mesh=mesh,
        in_specs=(
            P(None, "seq", "head"),
            P(None, "seq", "head"),
            P(None, "seq", "head"),
            P("seq", "head"),
            P("head", None),
            P("head", None, None),
            P("head", None, None),
            P("head", None, None),
            P("head"),
        ),
        out_specs=P(None, "seq", "head"),
        check_vma=False,
    )
```
